512 devices in a mesh: section: 64 (over z, y_hi, core), expert: 8 (over x, y_lo).
Axes of the slice: x: 4, y: 8 (y_hi: 4, y_lo: 2; y = y_hi * 2 + y_lo), z: 8, core: 2. Of those that a mesh axis runs over, the one named last changes fastest.
Arguments:
- grad_out: bfloat16 [64, 1024, 4096], P('section', 'expert'), may hold values from -6 to 6
- expert_outputs: bfloat16 [64, 2560, 4096], P('section', 'expert'), may hold values from -0.29882812 to 0.29882812
- expert_ids: int32 [64, 1024, 2], P('section', 'expert'), may hold values from 0 to 7, as said below
- bin_slots: int32 [64, 1024, 2], P('section', 'expert'), may hold values from 0 to 39, as said below
- keep_mask: int32 [64, 1024, 2], P('section', 'expert'), may hold values from 0 to 1
- router_logits: float32 [64, 1024, 8], P('section', 'expert'), may hold values from -9 to 9
- router_weight: bfloat16 [64, 4096, 8], P('section'), may hold values from -0.59765625 to 0.59765625
Outputs:
- passed_grad: bfloat16 [64, 1024, 4096], P('section', 'expert')
- router_grad: float32 [64, 1024, 8], P('section', 'expert')
The draws below stay inside these ranges and needn't reach their ends.
Inputs may be any that keep to these rules, and one draw needn't show every extreme that they name: `expert_ids`: the 2 experts of a token differ. `bin_slots`: among the kept choices of the tokens of one device, those of one expert hold distinct slots.
All inputs are finite; a program needn't handle non-finite values.
Results may differ from the reference program's by a relative error of at most 0.003.
Values may be sent and summed in bfloat16 or wider, within the bound.
A program may use at most 64 MiB of HBM per device.

```python
import jax
import jax.numpy as jnp
from jax import lax

D = 4096
TOP = 2
TOK_DEV = 128
EXPERTS = 8
CAPS = 40
TOKENS = 1024
SECTIONS = 64


def routing(key):
    blocks = SECTIONS * (TOKENS // TOK_DEV)
    hot_count = min(TOK_DEV, CAPS + TOK_DEV // 4)
    key_hot, key_rank, key_lead, key_other = jax.random.split(key, 4)
    hot_expert = jax.random.randint(key_hot, (blocks, 1), 0, EXPERTS)
    scores = jax.random.randint(key_rank, (blocks, TOK_DEV), 0, 1 << 20) * TOK_DEV + jnp.arange(TOK_DEV)[None, :]
    ranks = jnp.argsort(jnp.argsort(scores, axis=1, stable=True), axis=1, stable=True)
    lead_pick = jnp.where(ranks < hot_count, hot_expert, jax.random.randint(key_lead, (blocks, TOK_DEV), 0, EXPERTS))
    other_pick = (lead_pick + jax.random.randint(key_other, (blocks, TOK_DEV), 1, EXPERTS)) % EXPERTS
    picks = jnp.stack([lead_pick, other_pick], axis=2).reshape(blocks, TOK_DEV * TOP)
    onehot = (picks[:, :, None] == jnp.arange(EXPERTS)[None, None, :]).astype(jnp.int32)
    earlier = jnp.cumsum(onehot, axis=1) - onehot
    counts = jnp.sum(earlier * onehot, axis=2)
    return (picks, counts)


def distinct_order(key, shape, width):
    scores = jax.random.randint(key, shape + (width,), 0, 1 << 20) * width + jnp.arange(width)
    return jnp.argsort(scores, axis=-1, stable=True).astype(jnp.int32)


def draw_expert_ids(key, part):
    picks, counts = routing(key)
    key = jax.random.fold_in(key, 11)
    relabel = distinct_order(key, (picks.shape[0],), EXPERTS)
    labels = jnp.take_along_axis(relabel, picks, axis=1)
    return labels.reshape(SECTIONS, TOKENS, TOP).astype(jnp.int32)


def draw_bin_slots(key, part):
    picks, counts = routing(key)
    key = jax.random.fold_in(key, 23)
    blocks = picks.shape[0]
    order = distinct_order(key, (blocks, EXPERTS), CAPS)
    table = order[jnp.arange(blocks)[:, None], picks]
    slot_vals = jnp.take_along_axis(table, (counts % CAPS)[:, :, None], axis=2)[:, :, 0]
    return slot_vals.reshape(SECTIONS, TOKENS, TOP).astype(jnp.int32)


def draw_keep_mask(key, part):
    picks, counts = routing(key)
    key = jax.random.fold_in(key, 37)
    luck = jax.random.randint(key, counts.shape, 0, 8)
    kept = ((counts < CAPS) & (luck > 0)).astype(jnp.int32)
    return kept.reshape(SECTIONS, TOKENS, TOP)


def steps_of(rng, dims, cuts, low, top_value):
    def one(axis_at, parts):
        heights = jax.random.uniform(jax.random.fold_in(jax.random.fold_in(rng, 6), axis_at), (parts,), jnp.float32, low / len(cuts), top_value / len(cuts))
        return jnp.repeat(jnp.exp(heights), dims[axis_at] // parts).reshape((-1,) + (1,) * (len(dims) - axis_at - 1))

    level = one(*cuts[0])
    for cut in cuts[1:]:
        level = level * one(*cut)
    return level


def noise(key, dims, scale, most, shards=(), kind=jnp.bfloat16):
    entries = scale * jax.random.normal(key, dims, jnp.float32)
    if shards:
        entries = entries * steps_of(key, dims, shards, -0.22, 0.18)
    return jnp.clip(entries, -most, most).astype(kind)


def setup_inputs(seed: int = 0) -> dict:
    seeds = jax.random.split(jax.random.key(seed), 8)
    return {
        "grad_out": noise(seeds[0], (SECTIONS, TOKENS, D), 1.0, 6.0, ((0, 64), (1, 8))),
        "expert_outputs": noise(seeds[1], (SECTIONS, EXPERTS * EXPERTS * CAPS, D), 0.05, 0.29882812, ((0, 64), (1, 8))),
        "expert_ids": draw_expert_ids(jax.random.fold_in(seeds[7], 71), 0),
        "bin_slots": draw_bin_slots(jax.random.fold_in(seeds[7], 71), 0),
        "keep_mask": draw_keep_mask(jax.random.fold_in(seeds[7], 71), 0),
        "router_logits": noise(seeds[5], (SECTIONS, TOKENS, EXPERTS), 1.5, 9.0, ((0, 64), (1, 8)), jnp.float32),
        "router_weight": noise(seeds[6], (SECTIONS, D, EXPERTS), 0.1, 0.59765625, ((0, 64),)),
    }


def one_section(pieces):
    upstream, binned, routed, slot_ids, kept_mask, logits, weight = pieces
    source = (jnp.arange(TOKENS) // TOK_DEV).astype(jnp.int32)
    bin_rows = (routed * (EXPERTS * CAPS) + source[:, None] * CAPS + slot_ids).astype(jnp.int32)
    picked = binned[bin_rows.reshape(-1)].reshape(TOKENS, TOP, D)
    inner = jnp.einsum("nd,nkd->nk", upstream.astype(jnp.float32), picked.astype(jnp.float32))
    inner = inner * kept_mask.astype(jnp.float32)
    chosen = jnp.take_along_axis(logits, routed, axis=1)
    lead_gate = 1.0 / (1.0 + jnp.exp(chosen[:, 1] - chosen[:, 0]))
    gate_vals = jnp.stack([lead_gate, 1.0 - lead_gate], axis=1)
    gate_mean = jnp.sum(gate_vals * inner, axis=1, keepdims=True)
    chosen_grad = gate_vals * (inner - gate_mean)
    onehot = (routed[:, :, None] == jnp.arange(EXPERTS).astype(jnp.int32)[None, None, :]).astype(jnp.float32)
    logit_grad = jnp.sum(chosen_grad[:, :, None] * onehot, axis=1)
    router_term = jnp.dot(logit_grad, weight.astype(jnp.float32).T, precision=lax.Precision.HIGHEST)
    input_grad = (upstream.astype(jnp.float32) + router_term).astype(jnp.bfloat16)
    return input_grad, logit_grad


def reference(grad_out, expert_outputs, expert_ids, bin_slots, keep_mask, router_logits, router_weight):
    input_grad, logit_grad = lax.map(one_section, (grad_out, expert_outputs, expert_ids, bin_slots, keep_mask, router_logits, router_weight))
    return jnp.roll(input_grad, -1, axis=0), logit_grad
```

```python
import functools

import jax
import jax.numpy as jnp
from jax import lax
from jax.experimental import pallas as pl
from jax.experimental.pallas import tpu as pltpu
from jax.sharding import PartitionSpec as P

MESH = pl.DeviceIdType.MESH
CHUNKS = 8
F32 = jnp.float32
BF16 = jnp.bfloat16


def kernel(
    caps,
    sections,
    g_hbm,
    e_hbm,
    ids_hbm,
    slots_hbm,
    keep_hbm,
    logits_hbm,
    w_hbm,
    out_ref,
    rg_ref,
    g2,
    ebuf,
    grel,
    ids,
    slots,
    keep,
    logits,
    wrel,
    w3,
    code_own,
    code_par,
    coef,
    coef_rel,
    d_own,
    d_par,
    d_in,
    d_rel_a,
    d_rel_b,
    loc_sem,
    small_send,
    small_recv,
    e_send,
    e_recv,
    x_send,
    x_recv,
    r_send,
    r_recv,
):
    tok = g_hbm.shape[0]
    cols = g_hbm.shape[1]
    span = 2 * caps
    s = lax.axis_index("section")
    e = lax.axis_index("expert")
    core = lax.rem(s, 2)
    x = e // 2
    lo = lax.rem(e, 2)
    partner = (s, e + 1 - 2 * lo)
    before = lax.rem(s + sections - 1, sections)
    after = lax.rem(s + 1, sections)

    local = [
        pltpu.make_async_copy(ids_hbm, ids, loc_sem.at[0]),
        pltpu.make_async_copy(slots_hbm, slots, loc_sem.at[1]),
        pltpu.make_async_copy(keep_hbm, keep, loc_sem.at[2]),
        pltpu.make_async_copy(logits_hbm, logits, loc_sem.at[3]),
        pltpu.make_async_copy(g_hbm, g2.at[pl.ds(0, tok)], loc_sem.at[4]),
    ]
    mine = pl.ds(pl.multiple_of(x * span, 16), span)
    local.append(pltpu.make_async_copy(e_hbm.at[mine], ebuf.at[mine], loc_sem.at[5]))
    for copy in local:
        copy.start()

    barrier = pltpu.get_barrier_semaphore()
    peers = [(s, lax.rem(x + k, 4) * 2 + lo) for k in (1, 2, 3)]
    for source in peers + [partner, (after, e), (after, partner[1])]:
        pl.semaphore_signal(barrier, inc=1, device_id=source, device_id_type=MESH)
    pl.semaphore_wait(barrier, 6)

    def remote(src, dst, send, recv, device):
        return pltpu.make_async_remote_copy(
            src_ref=src, dst_ref=dst, send_sem=send, recv_sem=recv, device_id=device, device_id_type=MESH
        )

    rows = tok // CHUNKS
    exchange = [
        remote(
            g_hbm.at[pl.ds(i * rows, rows)],
            g2.at[pl.ds(tok + i * rows, rows)],
            x_send.at[i],
            x_recv.at[i],
            partner,
        )
        for i in range(CHUNKS)
    ]
    for copy in exchange:
        copy.start()
    experts = []
    for k, peer in enumerate(peers):
        theirs = pl.ds(pl.multiple_of(lax.rem(x + k + 1, 4) * span, 16), span)
        experts.append(remote(e_hbm.at[theirs], ebuf.at[mine], e_send.at[k], e_recv.at[k], peer))
        experts[-1].start()
    relay = remote(g_hbm, grel, r_send.at[0], r_recv, (before, e))
    direct = jnp.logical_or(core == 1, lo == 0)
    forwards = jnp.logical_and(core == 0, lo == 0)

    @pl.when(direct)
    def _():
        relay.start()

    weight = remote(w_hbm, wrel, small_send.at[0], small_recv.at[0], (before, e))
    weight.start()

    for copy in local[:4]:
        copy.wait()
    code = jnp.where(keep[...] > 0, ids[...] * caps + slots[...], -1)
    code_own[...] = code
    codes = remote(code_own, code_par, small_send.at[1], small_recv.at[1], partner)
    codes.start()
    experts_n = logits.shape[0]
    row = lax.broadcasted_iota(jnp.int32, (experts_n, tok), 0)
    first = (row == ids[0:1, :]).astype(F32)
    second = (row == ids[1:2, :]).astype(F32)
    gap = jnp.sum(logits[...] * (second - first), axis=0, keepdims=True)
    lead = 1.0 / (1.0 + jnp.exp(gap))
    coef[...] = lead * (1.0 - lead) * (first - second)
    coefs = remote(coef, coef_rel, small_send.at[2], small_recv.at[2], (before, e))
    coefs.start()

    for copy in local[4:]:
        copy.wait()
    forward = [
        remote(
            g2.at[pl.ds(tok + i * rows, rows)],
            grel.at[pl.ds(i * rows, rows)],
            r_send.at[i + 1],
            r_recv,
            (before, partner[1]),
        )
        for i in range(CHUNKS)
    ]
    for i in range(CHUNKS):
        exchange[i].wait_recv()

        @pl.when(forwards)
        def _():
            forward[i].start()

    weight.wait_recv()
    wide = wrel[...].astype(F32)
    w3[...] = jnp.concatenate([wide, wide, wide, jnp.zeros_like(wide)], axis=0).astype(BF16)
    codes.wait_recv()
    for copy in experts:
        copy.wait_recv()

    def part(first_row, codes_ref, tok_lo):
        sums = lax.dot_general(
            ebuf[...],
            g2[first_row : first_row + tok, :],
            (((1,), (1,)), ((), ())),
            preferred_element_type=F32,
        )
        total = jnp.zeros((1, tok), F32)
        for k in range(4):
            at = lax.broadcasted_iota(jnp.int32, (span, tok), 0) - tok_lo * caps
            inside = jnp.logical_and(at >= 0, at < caps)
            want = jnp.where(inside, at + (2 * k + lo) * caps, -2)
            block = sums[k * span : (k + 1) * span]
            total += jnp.sum(
                jnp.where(want == codes_ref[0:1, :], block, 0.0)
                - jnp.where(want == codes_ref[1:2, :], block, 0.0),
                axis=0,
                keepdims=True,
            )
        return jnp.broadcast_to(total, (8, tok))

    d_par[...] = part(tok, code_par, 1 - lo)
    back = remote(d_par, d_in, small_send.at[3], small_recv.at[3], partner)
    back.start()
    on = remote(d_par, d_rel_b, small_send.at[4], small_recv.at[4], (before, partner[1]))
    on.start()
    d_own[...] = part(0, code_own, lo)
    own = remote(d_own, d_rel_a, small_send.at[5], small_recv.at[5], (before, e))
    own.start()

    back.wait_recv()
    rg_ref[...] = coef[...] * (d_own[...] + d_in[...])

    coefs.wait_recv()
    on.wait_recv()
    own.wait_recv()
    grad = coef_rel[...] * (d_rel_a[...] + d_rel_b[...])
    high = grad.astype(BF16)
    rest = grad - high.astype(F32)
    mid = rest.astype(BF16)
    low = rest - mid.astype(F32)
    pieces = jnp.concatenate([high.astype(F32), mid.astype(F32), low, jnp.zeros_like(low)], axis=0)
    left = pieces.T.astype(BF16)
    relay.wait_recv()
    step = 512
    for at in range(0, cols, step):
        term = jnp.dot(left, w3[:, at : at + step], preferred_element_type=F32)
        out_ref[:, at : at + step] = (grel[:, at : at + step].astype(F32) + term).astype(BF16)

    for copy in exchange + experts + [weight, codes, coefs, back, on, own]:
        copy.wait_send()

    @pl.when(direct)
    def _():
        relay.wait_send()

    @pl.when(forwards)
    def _():
        for copy in forward:
            copy.wait_send()


def shards(
    grad_out, expert_outputs, expert_ids, bin_slots, keep_mask, router_logits, router_weight
):
    tok, cols = grad_out.shape[1:]
    experts_n = router_logits.shape[2]
    caps = expert_outputs.shape[1] // experts_n
    dma = pltpu.SemaphoreType.DMA
    passed, grad = pl.pallas_call(
        functools.partial(kernel, caps, lax.axis_size("section")),
        out_shape=(
            jax.ShapeDtypeStruct((tok, cols), BF16),
            jax.ShapeDtypeStruct((experts_n, tok), F32),
        ),
        in_specs=[pl.BlockSpec(memory_space=pltpu.HBM)] * 7,
        out_specs=(pl.BlockSpec(memory_space=pltpu.VMEM), pl.BlockSpec(memory_space=pltpu.VMEM)),
        scratch_shapes=[
            pltpu.VMEM((2 * tok, cols), BF16),
            pltpu.VMEM((8 * caps, cols), BF16),
            pltpu.VMEM((tok, cols), BF16),
            pltpu.VMEM((2, tok), jnp.int32),
            pltpu.VMEM((2, tok), jnp.int32),
            pltpu.VMEM((2, tok), jnp.int32),
            pltpu.VMEM((experts_n, tok), F32),
            pltpu.VMEM((experts_n, cols), BF16),
            pltpu.VMEM((4 * experts_n, cols), BF16),
            pltpu.VMEM((2, tok), jnp.int32),
            pltpu.VMEM((2, tok), jnp.int32),
            pltpu.VMEM((experts_n, tok), F32),
            pltpu.VMEM((experts_n, tok), F32),
            pltpu.VMEM((8, tok), F32),
            pltpu.VMEM((8, tok), F32),
            pltpu.VMEM((8, tok), F32),
            pltpu.VMEM((8, tok), F32),
            pltpu.VMEM((8, tok), F32),
            dma((6,)),
            dma((6,)),
            dma((6,)),
            dma((3,)),
            dma((3,)),
            dma((CHUNKS,)),
            dma((CHUNKS,)),
            dma((CHUNKS + 1,)),
            dma,
        ],
        compiler_params=pltpu.CompilerParams(
            collective_id=0, has_side_effects=True, vmem_limit_bytes=62 << 20
        ),
        cost_estimate=pl.CostEstimate(flops=700_000_000, bytes_accessed=8_000_000, transcendentals=128),
        name="combine_router_backward",
    )(
        grad_out[0],
        expert_outputs[0],
        expert_ids[0].T,
        bin_slots[0].T,
        keep_mask[0].T,
        router_logits[0].T,
        router_weight[0].T,
    )
    return (passed[None], grad.T[None])


def solution(mesh):
    in_specs = (
        P("section", "expert", None),
        P("section", "expert", None),
        P("section", "expert", None),
        P("section", "expert", None),
        P("section", "expert", None),
        P("section", "expert", None),
        P("section", None, None),
    )
    out_specs = (P("section", "expert", None), P("section", "expert", None))
    return jax.shard_map(shards, mesh=mesh, in_specs=in_specs, out_specs=out_specs, check_vma=False)
```

```python
import functools

import jax
import jax.numpy as jnp
from jax import lax
from jax.experimental import pallas as pl
from jax.experimental.pallas import tpu as pltpu
from jax.sharding import PartitionSpec as P

MESH = pl.DeviceIdType.MESH
CHUNKS = 8
FIRST = 2
SHARE = 3
LAUNCH = ((),(),(),(),(),(),(),(0,1,2,3,4,5,6,7))
F32 = jnp.float32
BF16 = jnp.bfloat16


def kernel(
    caps,
    sections,
    g_hbm,
    e_hbm,
    ids_hbm,
    slots_hbm,
    keep_hbm,
    logits_hbm,
    w_hbm,
    out_ref,
    rg_ref,
    g2,
    ebuf,
    grel,
    hbuf,
    e2,
    ids,
    slots,
    keep,
    logits,
    wrel,
    w3,
    code_own,
    code_par,
    coef,
    coef_rel,
    d_own,
    d_par,
    d_in,
    d_rel_a,
    d_rel_b,
    loc_sem,
    small_send,
    small_recv,
    e_send,
    e_recv,
    x_send,
    x_recv,
    r_send,
    o_send,
    r_recv,
    h_sem,
    c_send,
    c_recv,
    go_sem,
):
    tok = g_hbm.shape[0]
    cols = g_hbm.shape[1]
    span = 2 * caps
    s = lax.axis_index("section")
    e = lax.axis_index("expert")
    core = lax.rem(s, 2)
    x = e // 2
    lo = lax.rem(e, 2)
    partner = (s, e + 1 - 2 * lo)
    before = lax.rem(s + sections - 1, sections)
    after = lax.rem(s + 1, sections)

    barrier = pltpu.get_barrier_semaphore()
    peers = [(s, lax.rem(x + k, 4) * 2 + lo) for k in (1, 2, 3)]
    helper = jnp.logical_and(core == 1, lo == 0)
    helped = jnp.logical_and(core == 0, lo == 0)
    taker = jnp.logical_and(core == 1, lo == 1)
    across = [(s, lax.rem(x + k, 4) * 2 + 1 - lo) for k in (1, 2, 3)]
    behind = lax.rem(s + sections - 2, sections)

    def greet(devices, semaphore):
        for device in devices:
            pl.semaphore_signal(semaphore, inc=1, device_id=device, device_id_type=MESH)

    greet(peers + [partner], barrier)

    @pl.when(core == 0)
    def _():
        greet([(after, e), (after, partner[1]), (before, e), (before, partner[1])], barrier)
        pl.semaphore_wait(barrier, 4)

    @pl.when(core == 1)
    def _():
        @pl.when(lo == 0)
        def _():
            greet([(lax.rem(s + 2, sections), e)], barrier)
            pl.semaphore_wait(barrier, 12)
            greet([(before, e)], go_sem)

        @pl.when(lo == 1)
        def _():
            greet(across, barrier)
            pl.semaphore_wait(barrier, 8)

        greet([(after, e), (after, partner[1])], go_sem)

    local = [
        pltpu.make_async_copy(ids_hbm, ids, loc_sem.at[0]),
        pltpu.make_async_copy(slots_hbm, slots, loc_sem.at[1]),
        pltpu.make_async_copy(keep_hbm, keep, loc_sem.at[2]),
        pltpu.make_async_copy(logits_hbm, logits, loc_sem.at[3]),
        pltpu.make_async_copy(g_hbm, g2.at[pl.ds(0, tok)], loc_sem.at[4]),
    ]
    mine = pl.ds(pl.multiple_of(x * span, 16), span)
    local.append(pltpu.make_async_copy(e_hbm.at[mine], ebuf.at[mine], loc_sem.at[5]))
    for copy in local:
        copy.start()

    def remote(src, dst, send, recv, device):
        return pltpu.make_async_remote_copy(
            src_ref=src, dst_ref=dst, send_sem=send, recv_sem=recv, device_id=device, device_id_type=MESH
        )

    rows = tok // CHUNKS
    cut = cols // 8 * SHARE

    def swap(i, first):
        return remote(
            g_hbm.at[pl.ds(i * rows, rows), pl.ds(first, cols - first)],
            g2.at[pl.ds(tok + i * rows, rows), pl.ds(first, cols - first)],
            x_send.at[i],
            x_recv.at[i],
            partner,
        )

    exchange = [swap(i, 0) for i in range(CHUNKS)]
    shorter = [swap(i, cut) for i in range(CHUNKS)]

    @pl.when(taker)
    def _():
        for copy in shorter:
            copy.start()

    @pl.when(jnp.logical_not(taker))
    def _():
        for copy in exchange:
            copy.start()

    lead_rows = caps // 16 * 16 + 16

    def rows_to(k, first, count, from_col):
        theirs = pl.ds(pl.multiple_of(lax.rem(x + k + 1, 4) * span + first, 16), count)
        here = pl.ds(pl.multiple_of(x * span + first, 16), count)
        return remote(
            e_hbm.at[theirs, pl.ds(from_col, cols - from_col)],
            ebuf.at[here, pl.ds(from_col, cols - from_col)],
            e_send.at[k + (3 if first else 0)],
            e_recv.at[k + (3 if first else 0)],
            peers[k],
        )

    experts = [rows_to(k, 0, span, 0) for k in range(3)]
    experts_lead = [rows_to(k, 0, lead_rows, 0) for k in range(3)]
    experts_rest = [rows_to(k, lead_rows, span - lead_rows, cut) for k in range(3)]
    second = span - lead_rows

    def rows_across(k):
        at = x if k == 3 else lax.rem(x + k + 1, 4)
        return remote(
            e_hbm.at[pl.ds(pl.multiple_of(at * span + second, 16), lead_rows), pl.ds(0, cut)],
            e2.at[pl.ds(pl.multiple_of(x * lead_rows, 16), lead_rows)],
            c_send.at[k],
            c_recv.at[k],
            partner if k == 3 else across[k],
        )

    crossing = [rows_across(k) for k in range(4)]

    @pl.when(helper)
    def _():
        for copy in experts_lead + experts_rest + crossing:
            copy.start()

    @pl.when(jnp.logical_not(helper))
    def _():
        for copy in experts:
            copy.start()

    @pl.when(helped)
    def _():
        pl.semaphore_wait(go_sem, 3)

    @pl.when(jnp.logical_and(core == 0, lo == 1))
    def _():
        pl.semaphore_wait(go_sem, 2)

    relay = remote(g_hbm, grel, r_send.at[0], r_recv, (before, e))
    inside = core == 1
    help_out = remote(g_hbm, hbuf, h_sem.at[0], h_sem.at[1], (after, e))

    @pl.when(helped)
    def _():
        help_out.start()

    @pl.when(inside)
    def _():
        relay.start()

    weight = remote(w_hbm, wrel, small_send.at[0], small_recv.at[0], (before, e))
    weight.start()

    for copy in local[:4]:
        copy.wait()
    code = jnp.where(keep[...] > 0, ids[...] * caps + slots[...], -1)
    code_own[...] = code
    codes = remote(code_own, code_par, small_send.at[1], small_recv.at[1], partner)
    codes.start()
    experts_n = logits.shape[0]
    row = lax.broadcasted_iota(jnp.int32, (experts_n, tok), 0)
    first = (row == ids[0:1, :]).astype(F32)
    second_is = (row == ids[1:2, :]).astype(F32)
    gap = jnp.sum(logits[...] * (second_is - first), axis=0, keepdims=True)
    lead = 1.0 / (1.0 + jnp.exp(gap))
    coef[...] = lead * (1.0 - lead) * (first - second_is)
    coefs = remote(coef, coef_rel, small_send.at[2], small_recv.at[2], (before, e))
    coefs.start()

    for copy in local[4:]:
        copy.wait()
    forward = [
        remote(
            g2.at[pl.ds(tok + i * rows, rows)],
            grel.at[pl.ds(i * rows, rows)],
            r_send.at[i + 1],
            r_recv,
            (before, partner[1]),
        )
        for i in range(CHUNKS)
    ]
    outward = [
        remote(
            hbuf.at[pl.ds(i * rows, rows)],
            grel.at[pl.ds(i * rows, rows)],
            o_send.at[i],
            r_recv,
            (behind, e),
        )
        for i in range(CHUNKS)
    ]
    for i in range(CHUNKS):
        if i == FIRST:

            @pl.when(helper)
            def _():
                help_out.wait_recv()

        @pl.when(helper)
        def _():
            shorter[i].wait_recv()

        @pl.when(jnp.logical_not(helper))
        def _():
            exchange[i].wait_recv()

        @pl.when(helped)
        def _():
            forward[i].start()

        @pl.when(helper)
        def _():
            for j in LAUNCH[i]:
                outward[j].start()

    weight.wait_recv()
    wide = wrel[...].astype(F32)
    w3[...] = jnp.concatenate([wide, wide, wide, jnp.zeros_like(wide)], axis=0).astype(BF16)
    codes.wait_recv()

    d_own[...] = jnp.zeros_like(d_own)
    d_par[...] = jnp.zeros_like(d_par)

    def add(into, held, first_row, first_col, last_col, want, codes_ref):
        sums = lax.dot_general(
            held,
            g2[first_row : first_row + tok, first_col:last_col],
            (((1,), (1,)), ((), ())),
            preferred_element_type=F32,
        )
        total = jnp.sum(
            jnp.where(want == codes_ref[0:1, :], sums, 0.0)
            - jnp.where(want == codes_ref[1:2, :], sums, 0.0),
            axis=0,
            keepdims=True,
        )
        into[...] += jnp.broadcast_to(total, into.shape)

    def wanted(at, tok_lo):
        slot = lax.broadcasted_iota(jnp.int32, (span, tok), 0) - tok_lo * caps
        ours = jnp.logical_and(slot >= 0, slot < caps)
        return jnp.where(ours, slot + (2 * at + lo) * caps, -2)

    def block(at):
        here = pl.ds(pl.multiple_of(at * span, 16), span)
        add(d_own, ebuf[here, :], 0, 0, cols, wanted(at, lo), code_own)
        theirs = wanted(at, 1 - lo)
        add(d_par, ebuf[here, cut:], tok, cut, cols, theirs, code_par)

        @pl.when(jnp.logical_not(helper))
        def _():
            add(d_par, ebuf[here, :cut], tok, 0, cut, theirs, code_par)

    block(x)
    for k in (0, 2, 1):

        @pl.when(helper)
        def _():
            experts_lead[k].wait_recv()
            experts_rest[k].wait_recv()

        @pl.when(jnp.logical_not(helper))
        def _():
            experts[k].wait_recv()

        block(lax.rem(x + 3 - k, 4))

    @pl.when(taker)
    def _():
        for copy in crossing:
            copy.wait_recv()
        for at in range(4):
            slot = lax.broadcasted_iota(jnp.int32, (lead_rows, tok), 0) - (caps - second)
            want = jnp.where(slot >= 0, slot + 2 * at * caps, -2)
            add(d_own, e2[at * lead_rows : (at + 1) * lead_rows, :], 0, 0, cut, want, code_own)

    back = remote(d_par, d_in, small_send.at[3], small_recv.at[3], partner)
    back.start()
    on = remote(d_par, d_rel_b, small_send.at[4], small_recv.at[4], (before, partner[1]))
    on.start()
    own = remote(d_own, d_rel_a, small_send.at[5], small_recv.at[5], (before, e))
    own.start()

    back.wait_recv()
    rg_ref[...] = coef[...] * (d_own[...] + d_in[...])

    coefs.wait_recv()
    on.wait_recv()
    own.wait_recv()
    grad = coef_rel[...] * (d_rel_a[...] + d_rel_b[...])
    high = grad.astype(BF16)
    rest = grad - high.astype(F32)
    mid = rest.astype(BF16)
    low = rest - mid.astype(F32)
    pieces = jnp.concatenate([high.astype(F32), mid.astype(F32), low, jnp.zeros_like(low)], axis=0)
    left = pieces.T.astype(BF16)
    relay.wait_recv()
    step = 512
    for at in range(0, cols, step):
        term = jnp.dot(left, w3[:, at : at + step], preferred_element_type=F32)
        out_ref[:, at : at + step] = (grel[:, at : at + step].astype(F32) + term).astype(BF16)

    for copy in [weight, codes, coefs, back, on, own]:
        copy.wait_send()

    @pl.when(taker)
    def _():
        for copy in shorter:
            copy.wait_send()

    @pl.when(jnp.logical_not(taker))
    def _():
        for copy in exchange:
            copy.wait_send()

    @pl.when(helper)
    def _():
        for copy in experts_lead + experts_rest + crossing:
            copy.wait_send()

    @pl.when(jnp.logical_not(helper))
    def _():
        for copy in experts:
            copy.wait_send()

    @pl.when(inside)
    def _():
        relay.wait_send()

    @pl.when(helped)
    def _():
        for copy in forward + [help_out]:
            copy.wait_send()

    @pl.when(helper)
    def _():
        for copy in outward:
            copy.wait_send()


def shards(
    grad_out, expert_outputs, expert_ids, bin_slots, keep_mask, router_logits, router_weight
):
    tok, cols = grad_out.shape[1:]
    experts_n = router_logits.shape[2]
    caps = expert_outputs.shape[1] // experts_n
    dma = pltpu.SemaphoreType.DMA
    passed, grad = pl.pallas_call(
        functools.partial(kernel, caps, lax.axis_size("section")),
        out_shape=(
            jax.ShapeDtypeStruct((tok, cols), BF16),
            jax.ShapeDtypeStruct((experts_n, tok), F32),
        ),
        in_specs=[pl.BlockSpec(memory_space=pltpu.HBM)] * 7,
        out_specs=(pl.BlockSpec(memory_space=pltpu.VMEM), pl.BlockSpec(memory_space=pltpu.VMEM)),
        scratch_shapes=[
            pltpu.VMEM((2 * tok, cols), BF16),
            pltpu.VMEM((8 * caps, cols), BF16),
            pltpu.VMEM((tok, cols), BF16),
            pltpu.VMEM((tok, cols), BF16),
            pltpu.VMEM((4 * (caps // 16 * 16 + 16), cols // 8 * SHARE), BF16),
            pltpu.VMEM((2, tok), jnp.int32),
            pltpu.VMEM((2, tok), jnp.int32),
            pltpu.VMEM((2, tok), jnp.int32),
            pltpu.VMEM((experts_n, tok), F32),
            pltpu.VMEM((experts_n, cols), BF16),
            pltpu.VMEM((4 * experts_n, cols), BF16),
            pltpu.VMEM((2, tok), jnp.int32),
            pltpu.VMEM((2, tok), jnp.int32),
            pltpu.VMEM((experts_n, tok), F32),
            pltpu.VMEM((experts_n, tok), F32),
            pltpu.VMEM((8, tok), F32),
            pltpu.VMEM((8, tok), F32),
            pltpu.VMEM((8, tok), F32),
            pltpu.VMEM((8, tok), F32),
            pltpu.VMEM((8, tok), F32),
            dma((6,)),
            dma((6,)),
            dma((6,)),
            dma((6,)),
            dma((6,)),
            dma((CHUNKS,)),
            dma((CHUNKS,)),
            dma((CHUNKS + 1,)),
            dma((CHUNKS,)),
            dma,
            dma((2,)),
            dma((4,)),
            dma((4,)),
            pltpu.SemaphoreType.REGULAR,
        ],
        compiler_params=pltpu.CompilerParams(
            collective_id=0, has_side_effects=True, vmem_limit_bytes=40 << 20
        ),
        cost_estimate=pl.CostEstimate(flops=700_000_000, bytes_accessed=8_000_000, transcendentals=128),
        name="combine_router_backward",
    )(
        *(
            pltpu.with_memory_space_constraint(operand, pltpu.HBM)
            for operand in (
                grad_out[0],
                expert_outputs[0],
                expert_ids[0].T,
                bin_slots[0].T,
                keep_mask[0].T,
                router_logits[0].T,
                router_weight[0].T,
            )
        )
    )
    return (passed[None], grad.T[None])


def solution(mesh):
    in_specs = (
        P("section", "expert", None),
        P("section", "expert", None),
        P("section", "expert", None),
        P("section", "expert", None),
        P("section", "expert", None),
        P("section", "expert", None),
        P("section", None, None),
    )
    out_specs = (P("section", "expert", None), P("section", "expert", None))
    return jax.shard_map(shards, mesh=mesh, in_specs=in_specs, out_specs=out_specs, check_vma=False)
```

```python
import functools

import jax
import jax.numpy as jnp
from jax import lax
from jax.experimental import pallas as pl
from jax.experimental.pallas import tpu as pltpu
from jax.sharding import PartitionSpec as P

MESH = pl.DeviceIdType.MESH
CHUNKS = 8
FORWARD = 4
BESIDE = 3
FIRST = 5
SECOND = 5
SHARE = 1
F32 = jnp.float32
BF16 = jnp.bfloat16


def kernel(
    caps,
    sections,
    g_hbm,
    e_hbm,
    ids_hbm,
    slots_hbm,
    keep_hbm,
    logits_hbm,
    w_hbm,
    out_ref,
    rg_ref,
    g2,
    ebuf,
    grel,
    hbuf,
    e2,
    ids,
    slots,
    keep,
    logits,
    wrel,
    w3,
    code_all,
    coef,
    coef_rel,
    d_all,
    d_in,
    d_rel_a,
    d_rel_b,
    loc_sem,
    small_send,
    small_recv,
    e_send,
    e_recv,
    x_send,
    x_recv,
    r_send,
    r_recv,
    h_send,
    h_recv,
    c_send,
    c_recv,
    go_sem,
):
    tok = g_hbm.shape[0]
    cols = g_hbm.shape[1]
    span = 2 * caps
    s = lax.axis_index("section")
    e = lax.axis_index("expert")
    core = lax.rem(s, 2)
    x = e // 2
    lo = lax.rem(e, 2)
    partner = (s, e + 1 - 2 * lo)
    before = lax.rem(s + sections - 1, sections)
    after = lax.rem(s + 1, sections)

    barrier = pltpu.get_barrier_semaphore()
    peers = [(s, lax.rem(x + k, 4) * 2 + lo) for k in (1, 2, 3)]
    even = lo == 0
    c0_even, c0_odd = jnp.logical_and(core == 0, even), jnp.logical_and(core == 0, lo == 1)
    c1_even, c1_odd = jnp.logical_and(core == 1, even), jnp.logical_and(core == 1, lo == 1)
    across = [(s, lax.rem(x + k, 4) * 2 + 1 - lo) for k in (1, 2, 3)]

    def greet(devices, semaphore):
        for device in devices:
            pl.semaphore_signal(semaphore, inc=1, device_id=device, device_id_type=MESH)

    greet(peers + [partner], barrier)

    @pl.when(core == 0)
    def _():
        greet([(after, e), (after, partner[1]), (before, e), (before, partner[1])], barrier)
        pl.semaphore_wait(barrier, 4)

    @pl.when(core == 1)
    def _():
        @pl.when(lo == 1)
        def _():
            greet(across, barrier)
            pl.semaphore_wait(barrier, 8)

        @pl.when(even)
        def _():
            pl.semaphore_wait(barrier, 11)
            greet([(before, partner[1])], go_sem)

        greet([(after, e), (after, partner[1])], go_sem)

    local = [
        pltpu.make_async_copy(ids_hbm, ids, loc_sem.at[0]),
        pltpu.make_async_copy(slots_hbm, slots, loc_sem.at[1]),
        pltpu.make_async_copy(keep_hbm, keep, loc_sem.at[2]),
        pltpu.make_async_copy(logits_hbm, logits, loc_sem.at[3]),
        pltpu.make_async_copy(g_hbm, g2.at[pl.ds(0, tok)], loc_sem.at[4]),
    ]
    mine = pl.ds(pl.multiple_of(x * span, 16), span)
    local.append(pltpu.make_async_copy(e_hbm.at[mine], ebuf.at[mine], loc_sem.at[5]))
    for copy in local:
        copy.start()

    def remote(src, dst, send, recv, device):
        return pltpu.make_async_remote_copy(
            src_ref=src, dst_ref=dst, send_sem=send, recv_sem=recv, device_id=device, device_id_type=MESH
        )

    rows = tok // CHUNKS
    cut = cols // 8 * SHARE

    def swap(i, first):
        return remote(
            g_hbm.at[pl.ds(i * rows, rows), pl.ds(first, cols - first)],
            g2.at[pl.ds(tok + i * rows, rows), pl.ds(first, cols - first)],
            x_send.at[i],
            x_recv.at[i],
            partner,
        )

    exchange = [swap(i, 0) for i in range(CHUNKS)]
    shorter = [swap(i, cut) for i in range(CHUNKS)]

    @pl.when(c1_odd)
    def _():
        for copy in shorter:
            copy.start()

    @pl.when(jnp.logical_not(c1_odd))
    def _():
        for copy in exchange:
            copy.start()

    lead_rows = caps // 16 * 16 + 16

    def rows_to(k, first, count, from_col):
        theirs = pl.ds(pl.multiple_of(lax.rem(x + k + 1, 4) * span + first, 16), count)
        here = pl.ds(pl.multiple_of(x * span + first, 16), count)
        return remote(
            e_hbm.at[theirs, pl.ds(from_col, cols - from_col)],
            ebuf.at[here, pl.ds(from_col, cols - from_col)],
            e_send.at[k + (3 if first else 0)],
            e_recv.at[k + (3 if first else 0)],
            peers[k],
        )

    experts = [rows_to(k, 0, span, 0) for k in range(3)]
    experts_lead = [rows_to(k, 0, lead_rows, 0) for k in range(3)]
    experts_rest = [rows_to(k, lead_rows, span - lead_rows, cut) for k in range(3)]
    second = span - lead_rows

    def rows_across(k):
        at = x if k == 3 else lax.rem(x + k + 1, 4)
        return remote(
            e_hbm.at[pl.ds(pl.multiple_of(at * span + second, 16), lead_rows), pl.ds(0, cut)],
            e2.at[pl.ds(pl.multiple_of(x * lead_rows, 16), lead_rows)],
            c_send.at[k],
            c_recv.at[k],
            partner if k == 3 else across[k],
        )

    crossing = [rows_across(k) for k in range(4)]

    @pl.when(c1_even)
    def _():
        for copy in experts_lead + experts_rest + crossing:
            copy.start()

    @pl.when(jnp.logical_not(c1_even))
    def _():
        for copy in experts:
            copy.start()

    @pl.when(c0_even)
    def _():
        pl.semaphore_wait(go_sem, 2)

    @pl.when(c0_odd)
    def _():
        pl.semaphore_wait(go_sem, 3)

    relay = remote(g_hbm, grel, r_send.at[0], r_recv, (before, e))
    inside = core == 1
    half = tok // 2
    halves = [pl.ds(0, half), pl.ds(half, half)]
    hops = [
        remote(g_hbm.at[part], hbuf.at[part], h_send.at[k], h_recv.at[k], (before, partner[1]))
        for k, part in enumerate(halves)
    ]
    beside = remote(hbuf.at[halves[0]], hbuf.at[halves[0]], h_send.at[2], h_recv.at[2], (before, e))
    ends = [
        remote(hbuf.at[halves[1]], grel.at[halves[1]], h_send.at[3], r_recv, partner),
        remote(hbuf.at[halves[0]], grel.at[halves[0]], h_send.at[4], r_recv, (after, partner[1])),
    ]

    @pl.when(c0_even)
    def _():
        for copy in hops:
            copy.start()

    @pl.when(inside)
    def _():
        relay.start()

    weight = remote(w_hbm, wrel, small_send.at[0], small_recv.at[0], (before, e))
    weight.start()

    for copy in local[:4]:
        copy.wait()
    code = jnp.where(keep[...] > 0, ids[...] * caps + slots[...], -1)
    ours, theirs = pl.ds(0, tok), pl.ds(tok, tok)
    code_all[:, ours] = code
    codes = remote(code_all.at[:, ours], code_all.at[:, theirs], small_send.at[1], small_recv.at[1], partner)
    codes.start()
    experts_n = logits.shape[0]
    row = lax.broadcasted_iota(jnp.int32, (experts_n, tok), 0)
    first = (row == ids[0:1, :]).astype(F32)
    second_is = (row == ids[1:2, :]).astype(F32)
    gap = jnp.sum(logits[...] * (second_is - first), axis=0, keepdims=True)
    lead = 1.0 / (1.0 + jnp.exp(gap))
    coef[...] = lead * (1.0 - lead) * (first - second_is)
    coefs = remote(coef, coef_rel, small_send.at[2], small_recv.at[2], (before, e))
    coefs.start()

    for copy in local[4:]:
        copy.wait()
    d_all[...] = jnp.zeros_like(d_all)
    lane = lax.broadcasted_iota(jnp.int32, (span, 2 * tok), 1)
    slot = lax.broadcasted_iota(jnp.int32, (span, 2 * tok), 0) - jnp.where(lane < tok, lo, 1 - lo) * caps
    held_here = jnp.logical_and(slot >= 0, slot < caps)

    def wanted(at):
        return jnp.where(held_here, slot + (2 * at + lo) * caps, -2)

    def block_rows(at):
        return pl.ds(pl.multiple_of(at * span, 16), span)

    def product(held, first, last, first_col, last_col):
        return lax.dot_general(
            held, g2[first:last, first_col:last_col], (((1,), (1,)), ((), ())), preferred_element_type=F32
        )

    def pick(first, last, sums, want):
        total = jnp.sum(
            jnp.where(want == code_all[0:1, first:last], sums, 0.0)
            - jnp.where(want == code_all[1:2, first:last], sums, 0.0),
            axis=0,
            keepdims=True,
        )
        d_all[:, first:last] += jnp.broadcast_to(total, (8, last - first))

    def add(first, last, held, first_col, last_col, want):
        pick(first, last, product(held, first, last, first_col, last_col), want[:, first:last])

    def add_both(rows_at, want):
        @pl.when(c1_even)
        def _():
            add(0, 2 * tok, ebuf[rows_at, cut:], cut, cols, want)
            add(0, tok, ebuf[rows_at, :cut], 0, cut, want)

        @pl.when(jnp.logical_not(c1_even))
        def _():
            add(0, 2 * tok, ebuf[rows_at, :], 0, cols, want)

    add(0, tok, ebuf[block_rows(x), :], 0, cols, wanted(x))

    forward = [
        remote(
            g2.at[pl.ds(tok + i * rows, rows)],
            grel.at[pl.ds(i * rows, rows)],
            r_send.at[i + 1],
            r_recv,
            (before, partner[1]),
        )
        for i in range(CHUNKS)
    ]
    for i in range(CHUNKS):
        @pl.when(c1_even)
        def _():
            shorter[i].wait_recv()

        @pl.when(jnp.logical_not(c1_even))
        def _():
            exchange[i].wait_recv()


        if i == FORWARD:

            @pl.when(c0_even)
            def _():
                for copy in hops:
                    copy.wait_send()
                for copy in forward[: i + 1]:
                    copy.start()

        if i > FORWARD:

            @pl.when(c0_even)
            def _():
                forward[i].start()

        if i == BESIDE:

            @pl.when(c1_odd)
            def _():
                hops[0].wait_recv()
                beside.start()

        if i == FIRST:

            @pl.when(c1_odd)
            def _():
                hops[1].wait_recv()
                ends[0].start()

        if i == SECOND:

            @pl.when(c0_odd)
            def _():
                beside.wait_recv()
                ends[1].start()

    weight.wait_recv()
    wide = wrel[...].astype(F32)
    w3[...] = jnp.concatenate([wide, wide, wide, jnp.zeros_like(wide)], axis=0).astype(BF16)
    codes.wait_recv()


    here = block_rows(x)
    want = wanted(x)
    add(tok, 2 * tok, ebuf[here, cut:], cut, cols, want)

    @pl.when(jnp.logical_not(c1_even))
    def _():
        add(tok, 2 * tok, ebuf[here, :cut], 0, cut, want)

    for k in (0, 2, 1):

        @pl.when(c1_even)
        def _():
            experts_lead[k].wait_recv()
            experts_rest[k].wait_recv()

        @pl.when(jnp.logical_not(c1_even))
        def _():
            experts[k].wait_recv()

        at = lax.rem(x + 3 - k, 4)
        add_both(block_rows(at), wanted(at))

    @pl.when(c1_odd)
    def _():
        for copy in crossing:
            copy.wait_recv()
        sums = product(e2[...], 0, tok, 0, cut)
        slot = lax.broadcasted_iota(jnp.int32, (lead_rows, tok), 0) - (caps - second)
        for at in range(4):
            want = jnp.where(slot >= 0, slot + 2 * at * caps, -2)
            pick(0, tok, sums[at * lead_rows : (at + 1) * lead_rows], want)

    back = remote(d_all.at[:, theirs], d_in, small_send.at[3], small_recv.at[3], partner)
    back.start()
    on = remote(d_all.at[:, theirs], d_rel_b, small_send.at[4], small_recv.at[4], (before, partner[1]))
    on.start()
    own = remote(d_all.at[:, ours], d_rel_a, small_send.at[5], small_recv.at[5], (before, e))
    own.start()

    back.wait_recv()
    rg_ref[...] = coef[...] * (d_all[:, ours] + d_in[...])

    coefs.wait_recv()
    on.wait_recv()
    own.wait_recv()
    grad = coef_rel[...] * (d_rel_a[...] + d_rel_b[...])
    high = grad.astype(BF16)
    rest = grad - high.astype(F32)
    mid = rest.astype(BF16)
    low = rest - mid.astype(F32)
    pieces = jnp.concatenate([high.astype(F32), mid.astype(F32), low, jnp.zeros_like(low)], axis=0)
    left = pieces.T.astype(BF16)
    relay.wait_recv()
    step = 512
    for at in range(0, cols, step):
        term = jnp.dot(left, w3[:, at : at + step], preferred_element_type=F32)
        out_ref[:, at : at + step] = (grel[:, at : at + step].astype(F32) + term).astype(BF16)

    for copy in [weight, codes, coefs, back, on, own]:
        copy.wait_send()

    @pl.when(c1_odd)
    def _():
        for copy in shorter:
            copy.wait_send()

    @pl.when(jnp.logical_not(c1_odd))
    def _():
        for copy in exchange:
            copy.wait_send()

    @pl.when(c1_even)
    def _():
        for copy in experts_lead + experts_rest + crossing:
            copy.wait_send()

    @pl.when(jnp.logical_not(c1_even))
    def _():
        for copy in experts:
            copy.wait_send()

    @pl.when(inside)
    def _():
        relay.wait_send()

    @pl.when(c0_even)
    def _():
        for copy in forward:
            copy.wait_send()

    @pl.when(c1_odd)
    def _():
        beside.wait_send()
        ends[0].wait_send()

    @pl.when(c0_odd)
    def _():
        ends[1].wait_send()


def shards(
    grad_out, expert_outputs, expert_ids, bin_slots, keep_mask, router_logits, router_weight
):
    tok, cols = grad_out.shape[1:]
    experts_n = router_logits.shape[2]
    caps = expert_outputs.shape[1] // experts_n
    dma = pltpu.SemaphoreType.DMA
    passed, grad = pl.pallas_call(
        functools.partial(kernel, caps, lax.axis_size("section")),
        out_shape=(
            jax.ShapeDtypeStruct((tok, cols), BF16),
            jax.ShapeDtypeStruct((experts_n, tok), F32),
        ),
        in_specs=[pl.BlockSpec(memory_space=pltpu.HBM)] * 7,
        out_specs=(pl.BlockSpec(memory_space=pltpu.VMEM), pl.BlockSpec(memory_space=pltpu.VMEM)),
        scratch_shapes=[
            pltpu.VMEM((2 * tok, cols), BF16),
            pltpu.VMEM((8 * caps, cols), BF16),
            pltpu.VMEM((tok, cols), BF16),
            pltpu.VMEM((tok, cols), BF16),
            pltpu.VMEM((4 * (caps // 16 * 16 + 16), cols // 8 * SHARE), BF16),
            pltpu.VMEM((2, tok), jnp.int32),
            pltpu.VMEM((2, tok), jnp.int32),
            pltpu.VMEM((2, tok), jnp.int32),
            pltpu.VMEM((experts_n, tok), F32),
            pltpu.VMEM((experts_n, cols), BF16),
            pltpu.VMEM((4 * experts_n, cols), BF16),
            pltpu.VMEM((2, 2 * tok), jnp.int32),
            pltpu.VMEM((experts_n, tok), F32),
            pltpu.VMEM((experts_n, tok), F32),
            pltpu.VMEM((8, 2 * tok), F32),
            pltpu.VMEM((8, tok), F32),
            pltpu.VMEM((8, tok), F32),
            pltpu.VMEM((8, tok), F32),
            dma((6,)),
            dma((6,)),
            dma((6,)),
            dma((6,)),
            dma((6,)),
            dma((CHUNKS,)),
            dma((CHUNKS,)),
            dma((CHUNKS + 1,)),
            dma,
            dma((5,)),
            dma((3,)),
            dma((4,)),
            dma((4,)),
            pltpu.SemaphoreType.REGULAR,
        ],
        compiler_params=pltpu.CompilerParams(
            collective_id=0, has_side_effects=True, vmem_limit_bytes=40 << 20
        ),
        cost_estimate=pl.CostEstimate(flops=700_000_000, bytes_accessed=8_000_000, transcendentals=128),
        name="combine_router_backward",
    )(
        *(
            pltpu.with_memory_space_constraint(operand, pltpu.HBM)
            for operand in (
                grad_out[0],
                expert_outputs[0],
                expert_ids[0].T,
                bin_slots[0].T,
                keep_mask[0].T,
                router_logits[0].T,
                router_weight[0].T,
            )
        )
    )
    return (passed[None], grad.T[None])


def solution(mesh):
    in_specs = (
        P("section", "expert", None),
        P("section", "expert", None),
        P("section", "expert", None),
        P("section", "expert", None),
        P("section", "expert", None),
        P("section", "expert", None),
        P("section", None, None),
    )
    out_specs = (P("section", "expert", None), P("section", "expert", None))
    return jax.shard_map(shards, mesh=mesh, in_specs=in_specs, out_specs=out_specs, check_vma=False)
```

```python
import functools

import jax
import jax.numpy as jnp
from jax import lax
from jax.experimental import pallas as pl
from jax.experimental.pallas import tpu as pltpu
from jax.sharding import PartitionSpec as P

MESH = pl.DeviceIdType.MESH
CHUNKS = 8
FORWARD = 4
BESIDE = 3
FIRST = 5
SECOND = 5
SHARE = 1
PIECES = 4
F32 = jnp.float32
BF16 = jnp.bfloat16


def kernel(
    caps,
    sections,
    g_hbm,
    e_hbm,
    ids_hbm,
    slots_hbm,
    keep_hbm,
    logits_hbm,
    w_hbm,
    grel,
    w3,
    grad_ref,
    rg_ref,
    g2,
    ebuf,
    hbuf,
    e2,
    ids,
    slots,
    keep,
    logits,
    wrel,
    code_all,
    coef,
    coef_rel,
    d_all,
    d_in,
    d_rel_a,
    d_rel_b,
    loc_sem,
    small_send,
    small_recv,
    e_send,
    e_recv,
    x_send,
    x_recv,
    r_send,
    r_recv,
    h_send,
    h_recv,
    c_send,
    c_recv,
    go_sem,
):
    tok = g_hbm.shape[0]
    cols = g_hbm.shape[1]
    span = 2 * caps
    s = lax.axis_index("section")
    e = lax.axis_index("expert")
    core = lax.rem(s, 2)
    x = e // 2
    lo = lax.rem(e, 2)
    partner = (s, e + 1 - 2 * lo)
    before = lax.rem(s + sections - 1, sections)
    after = lax.rem(s + 1, sections)

    barrier = pltpu.get_barrier_semaphore()
    peers = [(s, lax.rem(x + k, 4) * 2 + lo) for k in (1, 2, 3)]
    even = lo == 0
    c0_even, c0_odd = jnp.logical_and(core == 0, even), jnp.logical_and(core == 0, lo == 1)
    c1_even, c1_odd = jnp.logical_and(core == 1, even), jnp.logical_and(core == 1, lo == 1)
    across = [(s, lax.rem(x + k, 4) * 2 + 1 - lo) for k in (1, 2, 3)]

    def greet(devices, semaphore):
        for device in devices:
            pl.semaphore_signal(semaphore, inc=1, device_id=device, device_id_type=MESH)

    greet(peers + [partner], barrier)

    @pl.when(core == 0)
    def _():
        greet([(after, e), (after, partner[1]), (before, e), (before, partner[1])], barrier)
        pl.semaphore_wait(barrier, 4)

    @pl.when(core == 1)
    def _():
        @pl.when(lo == 1)
        def _():
            greet(across, barrier)
            pl.semaphore_wait(barrier, 8)

        @pl.when(even)
        def _():
            pl.semaphore_wait(barrier, 11)
            greet([(before, partner[1])], go_sem)

        greet([(after, e), (after, partner[1])], go_sem)

    local = [
        pltpu.make_async_copy(ids_hbm, ids, loc_sem.at[0]),
        pltpu.make_async_copy(slots_hbm, slots, loc_sem.at[1]),
        pltpu.make_async_copy(keep_hbm, keep, loc_sem.at[2]),
        pltpu.make_async_copy(logits_hbm, logits, loc_sem.at[3]),
        pltpu.make_async_copy(g_hbm, g2.at[pl.ds(0, tok)], loc_sem.at[4]),
    ]
    mine = pl.ds(pl.multiple_of(x * span, 16), span)
    local.append(pltpu.make_async_copy(e_hbm.at[mine], ebuf.at[mine], loc_sem.at[5]))
    for copy in local:
        copy.start()

    def remote(src, dst, send, recv, device):
        return pltpu.make_async_remote_copy(
            src_ref=src, dst_ref=dst, send_sem=send, recv_sem=recv, device_id=device, device_id_type=MESH
        )

    rows = tok // CHUNKS
    cut = cols // 8 * SHARE

    def swap(i, first):
        return remote(
            g_hbm.at[pl.ds(i * rows, rows), pl.ds(first, cols - first)],
            g2.at[pl.ds(tok + i * rows, rows), pl.ds(first, cols - first)],
            x_send.at[i],
            x_recv.at[i],
            partner,
        )

    exchange = [swap(i, 0) for i in range(CHUNKS)]
    shorter = [swap(i, cut) for i in range(CHUNKS)]

    @pl.when(c1_odd)
    def _():
        for copy in shorter:
            copy.start()

    @pl.when(jnp.logical_not(c1_odd))
    def _():
        for copy in exchange:
            copy.start()

    lead_rows = caps // 16 * 16 + 16

    def rows_to(k, first, count, from_col):
        theirs = pl.ds(pl.multiple_of(lax.rem(x + k + 1, 4) * span + first, 16), count)
        here = pl.ds(pl.multiple_of(x * span + first, 16), count)
        return remote(
            e_hbm.at[theirs, pl.ds(from_col, cols - from_col)],
            ebuf.at[here, pl.ds(from_col, cols - from_col)],
            e_send.at[k + (3 if first else 0)],
            e_recv.at[k + (3 if first else 0)],
            peers[k],
        )

    experts = [rows_to(k, 0, span, 0) for k in range(3)]
    experts_lead = [rows_to(k, 0, lead_rows, 0) for k in range(3)]
    experts_rest = [rows_to(k, lead_rows, span - lead_rows, cut) for k in range(3)]
    second = span - lead_rows

    def rows_across(k):
        at = x if k == 3 else lax.rem(x + k + 1, 4)
        return remote(
            e_hbm.at[pl.ds(pl.multiple_of(at * span + second, 16), lead_rows), pl.ds(0, cut)],
            e2.at[pl.ds(pl.multiple_of(x * lead_rows, 16), lead_rows)],
            c_send.at[k],
            c_recv.at[k],
            partner if k == 3 else across[k],
        )

    crossing = [rows_across(k) for k in range(4)]

    @pl.when(c1_even)
    def _():
        for copy in experts_lead + experts_rest + crossing:
            copy.start()

    @pl.when(jnp.logical_not(c1_even))
    def _():
        for copy in experts:
            copy.start()

    @pl.when(c0_even)
    def _():
        pl.semaphore_wait(go_sem, 2)

    @pl.when(c0_odd)
    def _():
        pl.semaphore_wait(go_sem, 3)

    relay = remote(g_hbm, grel, r_send.at[0], r_recv, (before, e))
    inside = core == 1
    half = tok // 2
    halves = [pl.ds(0, half), pl.ds(half, half)]
    hops = [
        remote(g_hbm.at[part], hbuf.at[part], h_send.at[k], h_recv.at[k], (before, partner[1]))
        for k, part in enumerate(halves)
    ]
    beside = remote(hbuf.at[halves[0]], hbuf.at[halves[0]], h_send.at[2], h_recv.at[2], (before, e))
    ends = [
        remote(hbuf.at[halves[1]], grel.at[halves[1]], h_send.at[3], r_recv, partner),
        remote(hbuf.at[halves[0]], grel.at[halves[0]], h_send.at[4], r_recv, (after, partner[1])),
    ]

    @pl.when(c0_even)
    def _():
        for copy in hops:
            copy.start()

    @pl.when(inside)
    def _():
        relay.start()

    weight = remote(w_hbm, wrel, small_send.at[0], small_recv.at[0], (before, e))
    weight.start()

    for copy in local[:4]:
        copy.wait()
    code = jnp.where(keep[...] > 0, ids[...] * caps + slots[...], -1)
    ours, theirs = pl.ds(0, tok), pl.ds(tok, tok)
    code_all[:, ours] = code
    codes = remote(code_all.at[:, ours], code_all.at[:, theirs], small_send.at[1], small_recv.at[1], partner)
    codes.start()
    experts_n = logits.shape[0]
    row = lax.broadcasted_iota(jnp.int32, (experts_n, tok), 0)
    first = (row == ids[0:1, :]).astype(F32)
    second_is = (row == ids[1:2, :]).astype(F32)
    gap = jnp.sum(logits[...] * (second_is - first), axis=0, keepdims=True)
    lead = 1.0 / (1.0 + jnp.exp(gap))
    coef[...] = lead * (1.0 - lead) * (first - second_is)
    coefs = remote(coef, coef_rel, small_send.at[2], small_recv.at[2], (before, e))
    coefs.start()

    for copy in local[4:]:
        copy.wait()
    d_all[...] = jnp.zeros_like(d_all)
    lane = lax.broadcasted_iota(jnp.int32, (span, 2 * tok), 1)
    slot = lax.broadcasted_iota(jnp.int32, (span, 2 * tok), 0) - jnp.where(lane < tok, lo, 1 - lo) * caps
    held_here = jnp.logical_and(slot >= 0, slot < caps)

    def wanted(at):
        return jnp.where(held_here, slot + (2 * at + lo) * caps, -2)

    def block_rows(at):
        return pl.ds(pl.multiple_of(at * span, 16), span)

    def product(held, first, last, first_col, last_col):
        return lax.dot_general(
            held, g2[first:last, first_col:last_col], (((1,), (1,)), ((), ())), preferred_element_type=F32
        )

    def pick(first, last, sums, want):
        total = jnp.sum(
            jnp.where(want == code_all[0:1, first:last], sums, 0.0)
            - jnp.where(want == code_all[1:2, first:last], sums, 0.0),
            axis=0,
            keepdims=True,
        )
        d_all[:, first:last] += jnp.broadcast_to(total, (8, last - first))

    def add(first, last, held, first_col, last_col, want):
        pick(first, last, product(held, first, last, first_col, last_col), want[:, first:last])

    def add_both(rows_at, want):
        @pl.when(c1_even)
        def _():
            add(0, 2 * tok, ebuf[rows_at, cut:], cut, cols, want)
            add(0, tok, ebuf[rows_at, :cut], 0, cut, want)

        @pl.when(jnp.logical_not(c1_even))
        def _():
            add(0, 2 * tok, ebuf[rows_at, :], 0, cols, want)

    add(0, tok, ebuf[block_rows(x), :], 0, cols, wanted(x))

    forward = [
        remote(
            g2.at[pl.ds(tok + i * rows, rows)],
            grel.at[pl.ds(i * rows, rows)],
            r_send.at[i + 1],
            r_recv,
            (before, partner[1]),
        )
        for i in range(CHUNKS)
    ]
    for i in range(CHUNKS):
        @pl.when(c1_even)
        def _():
            shorter[i].wait_recv()

        @pl.when(jnp.logical_not(c1_even))
        def _():
            exchange[i].wait_recv()


        if i == FORWARD:

            @pl.when(c0_even)
            def _():
                for copy in hops:
                    copy.wait_send()
                for copy in forward[: i + 1]:
                    copy.start()

        if i > FORWARD:

            @pl.when(c0_even)
            def _():
                forward[i].start()

        if i == BESIDE:

            @pl.when(c1_odd)
            def _():
                hops[0].wait_recv()
                beside.start()

        if i == FIRST:

            @pl.when(c1_odd)
            def _():
                hops[1].wait_recv()
                ends[0].start()

        if i == SECOND:

            @pl.when(c0_odd)
            def _():
                beside.wait_recv()
                ends[1].start()

    weight.wait_recv()
    wide = wrel[...].astype(F32)
    w3[...] = jnp.concatenate([wide, wide, wide, jnp.zeros_like(wide)], axis=0).astype(BF16)
    codes.wait_recv()


    here = block_rows(x)
    want = wanted(x)
    add(tok, 2 * tok, ebuf[here, cut:], cut, cols, want)

    @pl.when(jnp.logical_not(c1_even))
    def _():
        add(tok, 2 * tok, ebuf[here, :cut], 0, cut, want)

    for k in (0, 2, 1):

        @pl.when(c1_even)
        def _():
            experts_lead[k].wait_recv()
            experts_rest[k].wait_recv()

        @pl.when(jnp.logical_not(c1_even))
        def _():
            experts[k].wait_recv()

        at = lax.rem(x + 3 - k, 4)
        add_both(block_rows(at), wanted(at))

    @pl.when(c1_odd)
    def _():
        for copy in crossing:
            copy.wait_recv()
        sums = product(e2[...], 0, tok, 0, cut)
        slot = lax.broadcasted_iota(jnp.int32, (lead_rows, tok), 0) - (caps - second)
        for at in range(4):
            want = jnp.where(slot >= 0, slot + 2 * at * caps, -2)
            pick(0, tok, sums[at * lead_rows : (at + 1) * lead_rows], want)

    back = remote(d_all.at[:, theirs], d_in, small_send.at[3], small_recv.at[3], partner)
    back.start()
    on = remote(d_all.at[:, theirs], d_rel_b, small_send.at[4], small_recv.at[4], (before, partner[1]))
    on.start()
    own = remote(d_all.at[:, ours], d_rel_a, small_send.at[5], small_recv.at[5], (before, e))
    own.start()

    back.wait_recv()
    rg_ref[...] = coef[...] * (d_all[:, ours] + d_in[...])

    coefs.wait_recv()
    on.wait_recv()
    own.wait_recv()
    grad_ref[...] = coef_rel[...] * (d_rel_a[...] + d_rel_b[...])
    relay.wait_recv()

    for copy in [weight, codes, coefs, back, on, own]:
        copy.wait_send()

    @pl.when(c1_odd)
    def _():
        for copy in shorter:
            copy.wait_send()

    @pl.when(jnp.logical_not(c1_odd))
    def _():
        for copy in exchange:
            copy.wait_send()

    @pl.when(c1_even)
    def _():
        for copy in experts_lead + experts_rest + crossing:
            copy.wait_send()

    @pl.when(jnp.logical_not(c1_even))
    def _():
        for copy in experts:
            copy.wait_send()

    @pl.when(inside)
    def _():
        relay.wait_send()

    @pl.when(c0_even)
    def _():
        for copy in forward:
            copy.wait_send()

    @pl.when(c1_odd)
    def _():
        beside.wait_send()
        ends[0].wait_send()

    @pl.when(c0_odd)
    def _():
        ends[1].wait_send()


def finish(rows_ref, w3, grad_ref, rg_ref, out_hbm, rg_hbm, out_ref, sem):
    cols = rows_ref.shape[1]
    rg_copy = pltpu.make_async_copy(rg_ref, rg_hbm, sem.at[PIECES])
    rg_copy.start()
    grad = grad_ref[...]
    high = grad.astype(BF16)
    rest = grad - high.astype(F32)
    mid = rest.astype(BF16)
    low = rest - mid.astype(F32)
    pieces = jnp.concatenate([high.astype(F32), mid.astype(F32), low, jnp.zeros_like(low)], axis=0)
    left = pieces.T.astype(BF16)
    step = cols // PIECES
    copies = []
    for k in range(PIECES):
        at = pl.ds(k * step, step)
        term = jnp.dot(left, w3[:, at], preferred_element_type=F32)
        out_ref[:, at] = (rows_ref[:, at].astype(F32) + term).astype(BF16)
        copies.append(pltpu.make_async_copy(out_ref.at[:, at], out_hbm.at[:, at], sem.at[k]))
        copies[-1].start()
    for copy in copies + [rg_copy]:
        copy.wait()


def shards(
    grad_out, expert_outputs, expert_ids, bin_slots, keep_mask, router_logits, router_weight
):
    tok, cols = grad_out.shape[1:]
    experts_n = router_logits.shape[2]
    caps = expert_outputs.shape[1] // experts_n
    dma = pltpu.SemaphoreType.DMA
    rows, w3, grad_next, grad_own = pl.pallas_call(
        functools.partial(kernel, caps, lax.axis_size("section")),
        out_shape=(
            jax.ShapeDtypeStruct((tok, cols), BF16),
            jax.ShapeDtypeStruct((4 * experts_n, cols), BF16),
            jax.ShapeDtypeStruct((experts_n, tok), F32),
            jax.ShapeDtypeStruct((experts_n, tok), F32),
        ),
        in_specs=[pl.BlockSpec(memory_space=pltpu.HBM)] * 7,
        out_specs=(pl.BlockSpec(memory_space=pltpu.VMEM),) * 4,
        scratch_shapes=[
            pltpu.VMEM((2 * tok, cols), BF16),
            pltpu.VMEM((8 * caps, cols), BF16),
            pltpu.VMEM((tok, cols), BF16),
            pltpu.VMEM((4 * (caps // 16 * 16 + 16), cols // 8 * SHARE), BF16),
            pltpu.VMEM((2, tok), jnp.int32),
            pltpu.VMEM((2, tok), jnp.int32),
            pltpu.VMEM((2, tok), jnp.int32),
            pltpu.VMEM((experts_n, tok), F32),
            pltpu.VMEM((experts_n, cols), BF16),
            pltpu.VMEM((2, 2 * tok), jnp.int32),
            pltpu.VMEM((experts_n, tok), F32),
            pltpu.VMEM((experts_n, tok), F32),
            pltpu.VMEM((8, 2 * tok), F32),
            pltpu.VMEM((8, tok), F32),
            pltpu.VMEM((8, tok), F32),
            pltpu.VMEM((8, tok), F32),
            dma((6,)),
            dma((6,)),
            dma((6,)),
            dma((6,)),
            dma((6,)),
            dma((CHUNKS,)),
            dma((CHUNKS,)),
            dma((CHUNKS + 1,)),
            dma,
            dma((5,)),
            dma((3,)),
            dma((4,)),
            dma((4,)),
            pltpu.SemaphoreType.REGULAR,
        ],
        compiler_params=pltpu.CompilerParams(
            collective_id=0, has_side_effects=True, vmem_limit_bytes=40 << 20
        ),
        cost_estimate=pl.CostEstimate(flops=700_000_000, bytes_accessed=8_000_000, transcendentals=128),
        name="combine_router_backward",
    )(
        *(
            pltpu.with_memory_space_constraint(operand, pltpu.HBM)
            for operand in (
                grad_out[0],
                expert_outputs[0],
                expert_ids[0].T,
                bin_slots[0].T,
                keep_mask[0].T,
                router_logits[0].T,
                router_weight[0].T,
            )
        )
    )
    passed, grad = pl.pallas_call(
        finish,
        out_shape=(
            jax.ShapeDtypeStruct((tok, cols), BF16),
            jax.ShapeDtypeStruct((experts_n, tok), F32),
        ),
        in_specs=[pl.BlockSpec(memory_space=pltpu.VMEM)] * 4,
        out_specs=(pl.BlockSpec(memory_space=pltpu.HBM),) * 2,
        scratch_shapes=[pltpu.VMEM((tok, cols), BF16), pltpu.SemaphoreType.DMA((PIECES + 1,))],
        compiler_params=pltpu.CompilerParams(vmem_limit_bytes=16 << 20),
        name="router_term",
    )(rows, w3, grad_next, grad_own)
    return (passed[None], grad.T[None])


def solution(mesh):
    in_specs = (
        P("section", "expert", None),
        P("section", "expert", None),
        P("section", "expert", None),
        P("section", "expert", None),
        P("section", "expert", None),
        P("section", "expert", None),
        P("section", None, None),
    )
    out_specs = (P("section", "expert", None), P("section", "expert", None))
    return jax.shard_map(shards, mesh=mesh, in_specs=in_specs, out_specs=out_specs, check_vma=False)
```

```python
import functools

import jax
import jax.numpy as jnp
from jax import lax
from jax.experimental import pallas as pl
from jax.experimental.pallas import tpu as pltpu
from jax.sharding import PartitionSpec as P

MESH = pl.DeviceIdType.MESH
CHUNKS = 8
ASIDE = 4
FORWARD = 4
BESIDE = 3
FIRST = 5
SECOND = 5
SHARE = 1
PIECES = 4
F32 = jnp.float32
BF16 = jnp.bfloat16


def kernel(
    caps,
    sections,
    g_hbm,
    e_hbm,
    ids_hbm,
    slots_hbm,
    keep_hbm,
    logits_hbm,
    w_hbm,
    grel,
    w3,
    grad_ref,
    rg_ref,
    g2,
    ebuf,
    hbuf,
    e2,
    ids,
    slots,
    keep,
    logits,
    wrel,
    code_all,
    coef,
    coef_rel,
    d_all,
    d_in,
    d_rel_a,
    d_rel_b,
    loc_sem,
    small_send,
    small_recv,
    e_send,
    e_recv,
    x_send,
    x_recv,
    r_send,
    r_recv,
    h_send,
    h_recv,
    c_send,
    c_recv,
    go_sem,
):
    tok = g_hbm.shape[0]
    cols = g_hbm.shape[1]
    span = 2 * caps
    s = lax.axis_index("section")
    e = lax.axis_index("expert")
    core = lax.rem(s, 2)
    x = e // 2
    lo = lax.rem(e, 2)
    partner = (s, e + 1 - 2 * lo)
    before = lax.rem(s + sections - 1, sections)
    after = lax.rem(s + 1, sections)

    barrier = pltpu.get_barrier_semaphore()
    peers = [(s, lax.rem(x + k, 4) * 2 + lo) for k in (1, 2, 3)]
    even = lo == 0
    c0_even, c0_odd = jnp.logical_and(core == 0, even), jnp.logical_and(core == 0, lo == 1)
    c1_even, c1_odd = jnp.logical_and(core == 1, even), jnp.logical_and(core == 1, lo == 1)
    across = [(s, lax.rem(x + k, 4) * 2 + 1 - lo) for k in (1, 2, 3)]

    def greet(devices, semaphore):
        for device in devices:
            pl.semaphore_signal(semaphore, inc=1, device_id=device, device_id_type=MESH)

    greet(peers + [partner], barrier)

    @pl.when(core == 0)
    def _():
        greet([(after, e), (after, partner[1]), (before, e), (before, partner[1])], barrier)
        pl.semaphore_wait(barrier, 4)

    @pl.when(core == 1)
    def _():
        @pl.when(lo == 1)
        def _():
            greet(across, barrier)
            pl.semaphore_wait(barrier, 8)

        @pl.when(even)
        def _():
            pl.semaphore_wait(barrier, 11)
            greet([(before, partner[1])], go_sem)

        greet([(after, e), (after, partner[1])], go_sem)

    local = [
        pltpu.make_async_copy(ids_hbm, ids, loc_sem.at[0]),
        pltpu.make_async_copy(slots_hbm, slots, loc_sem.at[1]),
        pltpu.make_async_copy(keep_hbm, keep, loc_sem.at[2]),
        pltpu.make_async_copy(logits_hbm, logits, loc_sem.at[3]),
        pltpu.make_async_copy(g_hbm, g2.at[pl.ds(0, tok)], loc_sem.at[4]),
    ]
    mine = pl.ds(pl.multiple_of(x * span, 16), span)
    local.append(pltpu.make_async_copy(e_hbm.at[mine], ebuf.at[mine], loc_sem.at[5]))
    for copy in local:
        copy.start()

    def remote(src, dst, send, recv, device):
        return pltpu.make_async_remote_copy(
            src_ref=src, dst_ref=dst, send_sem=send, recv_sem=recv, device_id=device, device_id_type=MESH
        )

    rows = tok // CHUNKS
    cut = cols // 8 * SHARE

    def swap(i, first):
        return remote(
            g_hbm.at[pl.ds(i * rows, rows), pl.ds(first, cols - first)],
            g2.at[pl.ds(tok + i * rows, rows), pl.ds(first, cols - first)],
            x_send.at[i],
            x_recv.at[i],
            partner,
        )

    exchange = [swap(i, 0) for i in range(CHUNKS)]
    shorter = [swap(i, cut) for i in range(CHUNKS)]

    @pl.when(c1_odd)
    def _():
        for copy in shorter:
            copy.start()

    @pl.when(jnp.logical_not(c1_odd))
    def _():
        for copy in exchange:
            copy.start()

    lead_rows = caps // 16 * 16 + 16

    def rows_to(k, first, count, from_col):
        theirs = pl.ds(pl.multiple_of(lax.rem(x + k + 1, 4) * span + first, 16), count)
        here = pl.ds(pl.multiple_of(x * span + first, 16), count)
        return remote(
            e_hbm.at[theirs, pl.ds(from_col, cols - from_col)],
            ebuf.at[here, pl.ds(from_col, cols - from_col)],
            e_send.at[k + (3 if first else 0)],
            e_recv.at[k + (3 if first else 0)],
            peers[k],
        )

    experts = [rows_to(k, 0, span, 0) for k in range(3)]
    experts_lead = [rows_to(k, 0, lead_rows, 0) for k in range(3)]
    experts_rest = [rows_to(k, lead_rows, span - lead_rows, cut) for k in range(3)]
    second = span - lead_rows

    def rows_across(k):
        at = x if k == 3 else lax.rem(x + k + 1, 4)
        return remote(
            e_hbm.at[pl.ds(pl.multiple_of(at * span + second, 16), lead_rows), pl.ds(0, cut)],
            e2.at[pl.ds(pl.multiple_of(x * lead_rows, 16), lead_rows)],
            c_send.at[k],
            c_recv.at[k],
            partner if k == 3 else across[k],
        )

    crossing = [rows_across(k) for k in range(4)]

    @pl.when(c1_even)
    def _():
        for copy in experts_lead + experts_rest + crossing:
            copy.start()

    @pl.when(jnp.logical_not(c1_even))
    def _():
        for copy in experts:
            copy.start()

    @pl.when(c0_even)
    def _():
        pl.semaphore_wait(go_sem, 2)

    @pl.when(c0_odd)
    def _():
        pl.semaphore_wait(go_sem, 3)

    relay = remote(g_hbm, grel, r_send.at[0], r_recv, (before, e))
    inside = core == 1
    half = tok // 2
    halves = [pl.ds(0, half), pl.ds(half, half)]
    hops = [
        remote(g_hbm.at[part], hbuf.at[part], h_send.at[k], h_recv.at[k], (before, partner[1]))
        for k, part in enumerate(halves)
    ]
    beside = remote(hbuf.at[halves[0]], hbuf.at[halves[0]], h_send.at[2], h_recv.at[2], (before, e))
    ends = [
        remote(hbuf.at[halves[1]], grel.at[halves[1]], h_send.at[3], r_recv, partner),
        remote(hbuf.at[halves[0]], grel.at[halves[0]], h_send.at[4], r_recv, (after, partner[1])),
    ]

    @pl.when(c0_even)
    def _():
        for copy in hops:
            copy.start()

    weight = remote(w_hbm, wrel, small_send.at[0], small_recv.at[0], (before, e))
    weight.start()

    for copy in local[:4]:
        copy.wait()
    code = jnp.where(keep[...] > 0, ids[...] * caps + slots[...], -1)
    ours, theirs = pl.ds(0, tok), pl.ds(tok, tok)
    code_all[:, ours] = code
    codes = remote(code_all.at[:, ours], code_all.at[:, theirs], small_send.at[1], small_recv.at[1], partner)
    codes.start()
    experts_n = logits.shape[0]
    row = lax.broadcasted_iota(jnp.int32, (experts_n, tok), 0)
    first = (row == ids[0:1, :]).astype(F32)
    second_is = (row == ids[1:2, :]).astype(F32)
    gap = jnp.sum(logits[...] * (second_is - first), axis=0, keepdims=True)
    lead = 1.0 / (1.0 + jnp.exp(gap))
    coef[...] = lead * (1.0 - lead) * (first - second_is)
    coefs = remote(coef, coef_rel, small_send.at[2], small_recv.at[2], (before, e))
    coefs.start()

    for copy in local[4:]:
        copy.wait()
    d_all[...] = jnp.zeros_like(d_all)
    lane = lax.broadcasted_iota(jnp.int32, (span, 2 * tok), 1)
    slot = lax.broadcasted_iota(jnp.int32, (span, 2 * tok), 0) - jnp.where(lane < tok, lo, 1 - lo) * caps
    held_here = jnp.logical_and(slot >= 0, slot < caps)

    def wanted(at):
        return jnp.where(held_here, slot + (2 * at + lo) * caps, -2)

    def block_rows(at):
        return pl.ds(pl.multiple_of(at * span, 16), span)

    def product(held, first, last, first_col, last_col):
        return lax.dot_general(
            held, g2[first:last, first_col:last_col], (((1,), (1,)), ((), ())), preferred_element_type=F32
        )

    def pick(first, last, sums, want):
        total = jnp.sum(
            jnp.where(want == code_all[0:1, first:last], sums, 0.0)
            - jnp.where(want == code_all[1:2, first:last], sums, 0.0),
            axis=0,
            keepdims=True,
        )
        d_all[:, first:last] += jnp.broadcast_to(total, (8, last - first))

    def add(first, last, held, first_col, last_col, want):
        pick(first, last, product(held, first, last, first_col, last_col), want[:, first:last])

    def add_both(rows_at, want):
        @pl.when(c1_even)
        def _():
            add(0, 2 * tok, ebuf[rows_at, cut:], cut, cols, want)
            add(0, tok, ebuf[rows_at, :cut], 0, cut, want)

        @pl.when(jnp.logical_not(c1_even))
        def _():
            add(0, 2 * tok, ebuf[rows_at, :], 0, cols, want)

    add(0, tok, ebuf[block_rows(x), :], 0, cols, wanted(x))

    forward = [
        remote(
            g2.at[pl.ds(tok + i * rows, rows)],
            grel.at[pl.ds(i * rows, rows)],
            r_send.at[i + 1],
            r_recv,
            (before, partner[1]),
        )
        for i in range(CHUNKS)
    ]
    for i in range(CHUNKS):
        @pl.when(c1_even)
        def _():
            shorter[i].wait_recv()

        @pl.when(jnp.logical_not(c1_even))
        def _():
            exchange[i].wait_recv()


        if i == FORWARD:

            @pl.when(c0_even)
            def _():
                for copy in hops:
                    copy.wait_send()
                for copy in forward[: i + 1]:
                    copy.start()

        if i > FORWARD:

            @pl.when(c0_even)
            def _():
                forward[i].start()

        if i == ASIDE:

            @pl.when(inside)
            def _():
                relay.start()

        if i == BESIDE:

            @pl.when(c1_odd)
            def _():
                hops[0].wait_recv()
                beside.start()

        if i == FIRST:

            @pl.when(c1_odd)
            def _():
                hops[1].wait_recv()
                ends[0].start()

        if i == SECOND:

            @pl.when(c0_odd)
            def _():
                beside.wait_recv()
                ends[1].start()

    weight.wait_recv()
    wide = wrel[...].astype(F32)
    w3[...] = jnp.concatenate([wide, wide, wide, jnp.zeros_like(wide)], axis=0).astype(BF16)
    codes.wait_recv()


    here = block_rows(x)
    want = wanted(x)
    add(tok, 2 * tok, ebuf[here, cut:], cut, cols, want)

    @pl.when(jnp.logical_not(c1_even))
    def _():
        add(tok, 2 * tok, ebuf[here, :cut], 0, cut, want)

    for k in (0, 2, 1):

        @pl.when(c1_even)
        def _():
            experts_lead[k].wait_recv()
            experts_rest[k].wait_recv()

        @pl.when(jnp.logical_not(c1_even))
        def _():
            experts[k].wait_recv()

        at = lax.rem(x + 3 - k, 4)
        add_both(block_rows(at), wanted(at))

    @pl.when(c1_odd)
    def _():
        for copy in crossing:
            copy.wait_recv()
        sums = product(e2[...], 0, tok, 0, cut)
        slot = lax.broadcasted_iota(jnp.int32, (lead_rows, tok), 0) - (caps - second)
        for at in range(4):
            want = jnp.where(slot >= 0, slot + 2 * at * caps, -2)
            pick(0, tok, sums[at * lead_rows : (at + 1) * lead_rows], want)

    back = remote(d_all.at[:, theirs], d_in, small_send.at[3], small_recv.at[3], partner)
    back.start()
    on = remote(d_all.at[:, theirs], d_rel_b, small_send.at[4], small_recv.at[4], (before, partner[1]))
    on.start()
    own = remote(d_all.at[:, ours], d_rel_a, small_send.at[5], small_recv.at[5], (before, e))
    own.start()

    back.wait_recv()
    rg_ref[...] = coef[...] * (d_all[:, ours] + d_in[...])

    coefs.wait_recv()
    on.wait_recv()
    own.wait_recv()
    grad_ref[...] = coef_rel[...] * (d_rel_a[...] + d_rel_b[...])
    relay.wait_recv()

    for copy in [weight, codes, coefs, back, on, own]:
        copy.wait_send()

    @pl.when(c1_odd)
    def _():
        for copy in shorter:
            copy.wait_send()

    @pl.when(jnp.logical_not(c1_odd))
    def _():
        for copy in exchange:
            copy.wait_send()

    @pl.when(c1_even)
    def _():
        for copy in experts_lead + experts_rest + crossing:
            copy.wait_send()

    @pl.when(jnp.logical_not(c1_even))
    def _():
        for copy in experts:
            copy.wait_send()

    @pl.when(inside)
    def _():
        relay.wait_send()

    @pl.when(c0_even)
    def _():
        for copy in forward:
            copy.wait_send()

    @pl.when(c1_odd)
    def _():
        beside.wait_send()
        ends[0].wait_send()

    @pl.when(c0_odd)
    def _():
        ends[1].wait_send()


def finish(rows_ref, w3, grad_ref, rg_ref, out_hbm, rg_hbm, out_ref, sem):
    cols = rows_ref.shape[1]
    rg_copy = pltpu.make_async_copy(rg_ref, rg_hbm, sem.at[PIECES])
    rg_copy.start()
    grad = grad_ref[...]
    high = grad.astype(BF16)
    rest = grad - high.astype(F32)
    mid = rest.astype(BF16)
    low = rest - mid.astype(F32)
    pieces = jnp.concatenate([high.astype(F32), mid.astype(F32), low, jnp.zeros_like(low)], axis=0)
    left = pieces.T.astype(BF16)
    step = cols // PIECES
    copies = []
    for k in range(PIECES):
        at = pl.ds(k * step, step)
        term = jnp.dot(left, w3[:, at], preferred_element_type=F32)
        out_ref[:, at] = (rows_ref[:, at].astype(F32) + term).astype(BF16)
        copies.append(pltpu.make_async_copy(out_ref.at[:, at], out_hbm.at[:, at], sem.at[k]))
        copies[-1].start()
    for copy in copies + [rg_copy]:
        copy.wait()


def shards(
    grad_out, expert_outputs, expert_ids, bin_slots, keep_mask, router_logits, router_weight
):
    tok, cols = grad_out.shape[1:]
    experts_n = router_logits.shape[2]
    caps = expert_outputs.shape[1] // experts_n
    dma = pltpu.SemaphoreType.DMA
    rows, w3, grad_next, grad_own = pl.pallas_call(
        functools.partial(kernel, caps, lax.axis_size("section")),
        out_shape=(
            jax.ShapeDtypeStruct((tok, cols), BF16),
            jax.ShapeDtypeStruct((4 * experts_n, cols), BF16),
            jax.ShapeDtypeStruct((experts_n, tok), F32),
            jax.ShapeDtypeStruct((experts_n, tok), F32),
        ),
        in_specs=[pl.BlockSpec(memory_space=pltpu.HBM)] * 7,
        out_specs=(pl.BlockSpec(memory_space=pltpu.VMEM),) * 4,
        scratch_shapes=[
            pltpu.VMEM((2 * tok, cols), BF16),
            pltpu.VMEM((8 * caps, cols), BF16),
            pltpu.VMEM((tok, cols), BF16),
            pltpu.VMEM((4 * (caps // 16 * 16 + 16), cols // 8 * SHARE), BF16),
            pltpu.VMEM((2, tok), jnp.int32),
            pltpu.VMEM((2, tok), jnp.int32),
            pltpu.VMEM((2, tok), jnp.int32),
            pltpu.VMEM((experts_n, tok), F32),
            pltpu.VMEM((experts_n, cols), BF16),
            pltpu.VMEM((2, 2 * tok), jnp.int32),
            pltpu.VMEM((experts_n, tok), F32),
            pltpu.VMEM((experts_n, tok), F32),
            pltpu.VMEM((8, 2 * tok), F32),
            pltpu.VMEM((8, tok), F32),
            pltpu.VMEM((8, tok), F32),
            pltpu.VMEM((8, tok), F32),
            dma((6,)),
            dma((6,)),
            dma((6,)),
            dma((6,)),
            dma((6,)),
            dma((CHUNKS,)),
            dma((CHUNKS,)),
            dma((CHUNKS + 1,)),
            dma,
            dma((5,)),
            dma((3,)),
            dma((4,)),
            dma((4,)),
            pltpu.SemaphoreType.REGULAR,
        ],
        compiler_params=pltpu.CompilerParams(
            collective_id=0, has_side_effects=True, vmem_limit_bytes=40 << 20
        ),
        cost_estimate=pl.CostEstimate(flops=700_000_000, bytes_accessed=8_000_000, transcendentals=128),
        name="combine_router_backward",
    )(
        *(
            pltpu.with_memory_space_constraint(operand, pltpu.HBM)
            for operand in (
                grad_out[0],
                expert_outputs[0],
                expert_ids[0].T,
                bin_slots[0].T,
                keep_mask[0].T,
                router_logits[0].T,
                router_weight[0].T,
            )
        )
    )
    passed, grad = pl.pallas_call(
        finish,
        out_shape=(
            jax.ShapeDtypeStruct((tok, cols), BF16),
            jax.ShapeDtypeStruct((experts_n, tok), F32),
        ),
        in_specs=[pl.BlockSpec(memory_space=pltpu.VMEM)] * 4,
        out_specs=(pl.BlockSpec(memory_space=pltpu.HBM),) * 2,
        scratch_shapes=[pltpu.VMEM((tok, cols), BF16), pltpu.SemaphoreType.DMA((PIECES + 1,))],
        compiler_params=pltpu.CompilerParams(vmem_limit_bytes=16 << 20),
        name="router_term",
    )(rows, w3, grad_next, grad_own)
    return (passed[None], grad.T[None])


def solution(mesh):
    in_specs = (
        P("section", "expert", None),
        P("section", "expert", None),
        P("section", "expert", None),
        P("section", "expert", None),
        P("section", "expert", None),
        P("section", "expert", None),
        P("section", None, None),
    )
    out_specs = (P("section", "expert", None), P("section", "expert", None))
    return jax.shard_map(shards, mesh=mesh, in_specs=in_specs, out_specs=out_specs, check_vma=False)
```
